128 devices in a mesh: comp: 2 (over core), dom: 64 (over z, y, x).
Axes of the slice: x: 4, y: 4, z: 4, core: 2. Of those that a mesh axis runs over, the one named last changes fastest.
Arguments:
- state: bfloat16 [4, 64, 131072], P(None, None, ('comp', 'dom')), may hold values from -6 to 6
- links: int32 [8, 131072], P(None, ('comp', 'dom')), may hold values from -512 to 512, as said below
- link_weight: float32 [8, 131072], P(None, ('comp', 'dom')), may hold values from 0 to 0.4, as said below
- point_mass: float32 [131072], P(('comp', 'dom')), may hold values from 2 to 8
- flow: float32 [2, 131072], P(None, ('comp', 'dom')), may hold values from -1 to 1
- ov_src: int32 [1048576], P(('comp', 'dom')), may hold values from 0 to 1023
- ov_owner: int32 [1048576, 1], P(('comp', 'dom')), may hold values from 0 to 63; in each aligned block of 8192 rows (0 to 8191, 8192 to 16383, ...) at most 512 rows name the same one
- ov_row: int32 [1048576], P(('comp', 'dom')), may hold values from 0 to 1023
- ov_weight: float32 [1048576], P(('comp', 'dom')), may hold values from 0.2 to 0.6
Outputs:
- new_state: bfloat16 [4, 64, 131072], P(None, None, ('comp', 'dom'))
- surface_import: float32 [4, 131072], P(None, ('comp', 'dom'))
The draws below stay inside these ranges and needn't reach their ends.
Inputs may be any that keep to these rules, and one draw needn't show every extreme that they name: The first 1 to 3 slots (atmosphere) or 5 to 7 slots (ocean) of a column are real links; the remaining slots are 0. `link_weight`: zero exactly on the padding slots. `ov_owner`: within the 8192 entries of one device no owner is named more than 512 times, a bound that some block reaches.
All inputs are finite; a program needn't handle non-finite values.
Results may differ from the reference program's by a relative error of at most 0.0065.
Values may be sent and summed in bfloat16 or wider, within the bound.
A program may use at most 128 MiB of HBM per device.

```python
import math
import jax
import jax.numpy as jnp
import numpy as np
from jax import lax

CH = 4
LEV = 64
K = 8
STEPS = 2
HW = 512
ROWS = 1024
OV = 8192
OWNERS = 64
COLS = 65536
ALL_COLS = 131072
NOV = 1048576
CAP = 512
N_DOM = 64


def link_counts(key):
    count_key = jax.random.fold_in(key, 101)
    atmosphere = jax.random.randint(count_key, (ALL_COLS,), 1, 4)
    ocean_side = jax.random.randint(jax.random.fold_in(count_key, 1), (ALL_COLS,), 5, 8)
    in_ocean = jnp.arange(ALL_COLS, dtype=jnp.int32) >= COLS
    return jnp.where(in_ocean, ocean_side, atmosphere)


def draw_links(key, part):
    counts = link_counts(key)
    key = jax.random.fold_in(key, 3)
    shifts = jax.random.randint(key, (K, ALL_COLS), -HW, HW + 1)
    slot_index = jnp.arange(K, dtype=jnp.int32)[:, None]
    return jnp.where(slot_index < counts[None, :], shifts, 0).astype(jnp.int32)


def draw_link_weight(key, part):
    counts = link_counts(key)
    key = jax.random.fold_in(key, 5)
    weights = jax.random.uniform(key, (K, ALL_COLS), jnp.float32, 0.1, 0.4)
    slot_index = jnp.arange(K, dtype=jnp.int32)[:, None]
    return jnp.where(slot_index < counts[None, :], weights, 0.0).astype(jnp.float32)


def touch_ends(entries, stream_key, smallest, top_value):
    dims = entries.shape
    index_at = [jax.random.randint(jax.random.fold_in(stream_key, axis), (), 0, dims[axis]) for axis in range(len(dims))]
    entries = entries.at[tuple(index_at)].set(smallest)
    longest = dims.index(max(dims))
    index_at[longest] = (index_at[longest] + 1) % dims[longest]
    return entries.at[tuple(index_at)].set(top_value)


def block_levels(own_key, extent, cuts, low, top_value):
    loudness = 1.0
    for axis_at, parts in cuts:
        steps = jax.random.uniform(jax.random.fold_in(jax.random.fold_in(own_key, 6), axis_at), (parts,), jnp.float32, low / len(cuts), top_value / len(cuts))
        loudness = loudness * jnp.repeat(jnp.exp(steps), extent[axis_at] // parts).reshape((-1,) + (1,) * (len(extent) - 1 - axis_at))
    return loudness


def routed_block(key, own, number, rows, amount, top, bound, skew):
    order = jax.random.permutation(key, amount)
    packed, ordinary = load_shares(amount, rows * top, bound, skew, True), load_shares(amount, rows * top, bound, skew, False)
    places = jnp.arange(amount)

    def named(sizes, offset_by):
        used = int((sizes > 0).sum())
        fixed = max(1, used // 4)
        moved = fixed + (places - fixed + offset_by * (used - fixed)) % max(1, amount - fixed)
        return jnp.zeros((amount,), jnp.int32).at[order[jnp.where(places < fixed, places, moved)]].set(jnp.asarray(sizes, jnp.int32))

    sizes = jnp.where(number % 4 == 0, named(packed, number // 4), named(ordinary, number - number // 4 - 1))
    mixed = jax.random.permutation(jax.random.fold_in(own, 3), amount)
    donor, sink = mixed[0:amount // 2 * 2:2], mixed[1:amount // 2 * 2:2]
    slack = jnp.minimum(sizes[donor] - 1, bound - sizes[sink]) // 2
    slack = jnp.where((donor == order[0]) | (sink == order[0]) | (sizes[sink] == 0), 0, jnp.maximum(slack, 0))
    moved = jax.random.randint(jax.random.fold_in(own, 4), (amount // 2,), 0, 1 << 20) % (slack + 1)
    sizes = sizes.at[donor].add(-moved).at[sink].add(moved)
    labels = jnp.searchsorted(jnp.cumsum(sizes), jnp.arange(rows * top), side="right").astype(jnp.int32)
    listing = labels.reshape(top, rows).T
    listing = listing[jax.random.permutation(jax.random.fold_in(own, 1), rows)]
    offset_by = jax.random.randint(jax.random.fold_in(own, 2), (rows, 1), 0, top)
    return jnp.take_along_axis(listing, (jnp.arange(top)[None, :] + offset_by) % top, axis=1)


def load_shares(count, total, bound, slope, full):
    weights = [(1 << 20) // math.isqrt(grade ** slope) + 1 for grade in range(1, count + 1)]
    largest = bound if full else min(bound, max(-(-total // count), total * weights[0] // sum(weights)))
    least = 1 if total - largest >= count - 1 else 0
    given, rest = [largest] + [least] * (count - 1), total - largest - least * (count - 1)
    while rest > 0:
        movable = [i for i in range(1, count) if given[i] < largest] or [i for i in range(1, count) if given[i] < bound]
        whole, remaining = sum([weights[i] for i in movable]), rest
        for i in movable:
            addition = min(bound - given[i], max(1, remaining * weights[i] // whole), rest)
            given[i] = given[i] + addition
            rest = rest - addition
    return np.array(given)


def bell_draw(own_key, dims, deviation, reach, split=(), held_as=jnp.bfloat16):
    result = deviation * jax.random.normal(own_key, dims, jnp.float32)
    if split:
        result = result * block_levels(own_key, dims, split, -0.22, 0.18)
    return jnp.clip(result, -reach, reach).astype(held_as)


def setup_inputs(seed: int = 0) -> dict:
    arg_keys = jax.random.split(jax.random.key(seed), 10)
    state = bell_draw(arg_keys[0], (CH, LEV, ALL_COLS), 1.0, 6.0, ((2, 128),))
    links = draw_links(jax.random.fold_in(arg_keys[9], 71), 0)
    link_weight = draw_link_weight(jax.random.fold_in(arg_keys[9], 71), 0)
    point_mass = jnp.clip(jnp.exp(math.log(8.0) - 1.3862944 * jax.random.uniform(arg_keys[3], (ALL_COLS,), jnp.float32) ** block_levels(arg_keys[3], (ALL_COLS,), ((0, 128),), -0.2, 0.2)), 2.0, 8.0)
    flow = jnp.clip(jax.random.uniform(arg_keys[4], (2, ALL_COLS), jnp.float32, -1.0, 1.0) * block_levels(arg_keys[4], (2, ALL_COLS), ((1, 128),), -0.4, 0.0), -1.0, 1.0)
    ov_src = touch_ends(jax.random.randint(arg_keys[5], (NOV,), 0, ROWS), jax.random.fold_in(arg_keys[5], 1), 0, ROWS - 1).astype(jnp.int32)
    ov_owner_keys = jax.random.split(jax.random.fold_in(arg_keys[6], 1), NOV // OV)
    ov_owner_turns = jax.random.permutation(jax.random.fold_in(arg_keys[6], 3), NOV // OV)
    ov_owner = jax.vmap(lambda own, number: routed_block(jax.random.fold_in(arg_keys[6], 2), own, number, OV, OWNERS, 1, CAP, 2))(ov_owner_keys, ov_owner_turns).reshape((NOV, 1))
    ov_row = touch_ends(jax.random.randint(arg_keys[7], (NOV,), 0, ROWS), jax.random.fold_in(arg_keys[7], 1), 0, ROWS - 1).astype(jnp.int32)
    ov_weight = jnp.clip(0.2 + 0.400000021 * jax.random.uniform(arg_keys[8], (NOV,), jnp.float32) ** block_levels(arg_keys[8], (NOV,), ((0, 128),), -0.2, 0.2), 0.2, 0.6)
    return dict(state=state, links=links, link_weight=link_weight, point_mass=point_mass, flow=flow, ov_src=ov_src, ov_owner=ov_owner, ov_row=ov_row, ov_weight=ov_weight)


DT_ATM = 0.04
DT_OCN = 0.5
COUPLE = 0.5
VMIX = 0.25

def derivative_tables():
    node_points = np.array([-1.0, -1.0 / math.sqrt(5.0), 1.0 / math.sqrt(5.0), 1.0])
    weights = np.ones(4)
    for column in range(4):
        for middle in range(4):
            if middle != column:
                weights[column] = weights[column] / (node_points[column] - node_points[middle])
    derivative = np.zeros((4, 4))
    for target in range(4):
        for column in range(4):
            if column != target:
                derivative[target, column] = weights[column] / weights[target] / (node_points[target] - node_points[column])
        derivative[target, target] = -np.sum(derivative[target])
    along_x = np.kron(np.eye(4), derivative)
    along_y = np.kron(derivative, np.eye(4))
    return (jnp.asarray(along_x, jnp.float32), jnp.asarray(along_y, jnp.float32))

def atm_advance(field, winds):
    along_x, along_y = derivative_tables()
    values = field.astype(jnp.float32)
    shaped = values.reshape(values.shape[0], values.shape[1], -1, 16)
    slope_x = jnp.einsum('clep,qp->cleq', shaped, along_x, precision=lax.Precision.HIGHEST).reshape(values.shape)
    slope_y = jnp.einsum('clep,qp->cleq', shaped, along_y, precision=lax.Precision.HIGHEST).reshape(values.shape)
    return (values - DT_ATM * (winds[0] * slope_x + winds[1] * slope_y)).astype(jnp.bfloat16)

def atm_average(own, source, positions, link_weight, mass):
    own_values = own.astype(jnp.float32)
    total = mass * own_values
    weight_sum = mass
    for slot in range(link_weight.shape[0]):
        total = total + link_weight[slot] * jnp.take(source, positions[slot], axis=2).astype(jnp.float32)
        weight_sum = weight_sum + link_weight[slot]
    return (total / weight_sum).astype(jnp.bfloat16)

def ocn_diffuse(own, source, positions, link_weight, area, winds):
    values = own.astype(jnp.float32)
    spread = jnp.zeros_like(values)
    for slot in range(link_weight.shape[0]):
        spread = spread + link_weight[slot] * (jnp.take(source, positions[slot], axis=2).astype(jnp.float32) - values)
    mixing = VMIX * winds[0] * winds[0]
    step_diff = values[:, 1:] - values[:, :-1]
    edge_zero = jnp.zeros_like(values[:, :1])
    upper = jnp.concatenate([step_diff, edge_zero], axis=1)
    lower = jnp.concatenate([edge_zero, step_diff], axis=1)
    return (values + DT_OCN * spread / area + mixing * (upper - lower)).astype(jnp.bfloat16)

def reference(state, links, link_weight, point_mass, flow, ov_src, ov_owner, ov_row, ov_weight):
    values = state.astype(jnp.float32)
    export = values[:, 0, :]
    entry_index = jnp.arange(ov_src.shape[0], dtype=jnp.int32)
    device_index = entry_index // OV
    group_index = device_index // N_DOM
    source_row = device_index * ROWS + ov_src
    target_row = (1 - group_index) * COLS + ov_owner[:, 0] * ROWS + ov_row
    contrib = ov_weight[None, :] * jnp.take(export, source_row, axis=1)
    surface_import = jnp.zeros_like(export).at[:, target_row].add(contrib)
    forced = values.at[:, 0, :].set(export + COUPLE * (surface_import - export)).astype(jnp.bfloat16)
    within = jnp.arange(COLS, dtype=jnp.int32)[None, :]
    atm_positions = ((within + links[:, :COLS]) % COLS).astype(jnp.int32)
    ocn_positions = ((within + links[:, COLS:]) % COLS).astype(jnp.int32)
    current = forced
    for stepno in range(STEPS):
        atmosphere = current[:, :, :COLS]
        ocean_part = current[:, :, COLS:]
        advanced = atm_advance(atmosphere, flow[:, :COLS])
        atmosphere = atm_average(advanced, advanced, atm_positions, link_weight[:, :COLS], point_mass[:COLS])
        ocean_part = ocn_diffuse(ocean_part, ocean_part, ocn_positions, link_weight[:, COLS:], point_mass[COLS:], flow[:, COLS:])
        current = jnp.concatenate([atmosphere, ocean_part], axis=2)
    return (current, surface_import)
```

```python
import functools
import math

import jax
import jax.numpy as jnp
import numpy as np
from jax import lax
from jax.experimental import pallas as pl
from jax.experimental.pallas import tpu as pltpu
from jax.sharding import PartitionSpec as P

CH = 4
LEV = 64
ROWS = 1024
HW = 512
BLK = 256
NB = ROWS // BLK
SPAN = BLK + 2 * HW
OWNERS = 64
ENT = 8192
SLAB = 1024
TAIL = 16
MESH = pl.DeviceIdType.MESH
BF = jnp.bfloat16
F32 = jnp.float32


def derivative():
    nodes = np.array([-1.0, -1.0 / math.sqrt(5.0), 1.0 / math.sqrt(5.0), 1.0])
    weights = np.ones(4)
    for column in range(4):
        for middle in range(4):
            if middle != column:
                weights[column] = weights[column] / (nodes[column] - nodes[middle])
    table = np.zeros((4, 4))
    for target in range(4):
        for column in range(4):
            if column != target:
                table[target, column] = weights[column] / weights[target] / (nodes[target] - nodes[column])
        table[target, target] = -np.sum(table[target])
    return table


def constants():
    d = derivative()
    along_x = np.kron(np.eye(4), d)
    along_y = np.kron(d, np.eye(4))
    kx = -0.04 * np.kron(np.eye(BLK // 16), along_x.T)
    ky = -0.04 * np.kron(np.eye(BLK // 16), along_y.T)
    kxy = np.stack([kx, ky])
    second = np.zeros((LEV, LEV))
    for l in range(LEV):
        if l + 1 < LEV:
            second[l, l + 1] += 1.0
            second[l, l] -= 1.0
        if l > 0:
            second[l, l - 1] += 1.0
            second[l, l] -= 1.0
    vert = np.kron(np.eye(CH), second)
    pick = np.zeros((TAIL, CH * LEV))
    place = np.zeros((CH, TAIL, TAIL))
    tvert = np.zeros((TAIL, TAIL))
    for lev in range(4):
        for ch in range(CH):
            r = lev * 4 + ch
            pick[r, ch * LEV + lev] = 1.0
            place[ch, lev, r] = 1.0
            for other in range(4):
                tvert[r, other * 4 + ch] = second[lev, other]
    return (
        jnp.asarray(kxy, BF),
        jnp.asarray(vert, BF),
        jnp.asarray(pick, BF),
        jnp.asarray(place.reshape(CH * TAIL, TAIL), BF),
        jnp.asarray(tvert, BF),
    )


def dot(a, b):
    return lax.dot_general(a, b, (((1,), (0,)), ((), ())), preferred_element_type=F32)


def dot_t(a, b):
    return lax.dot_general(a, b, (((1,), (1,)), ((), ())), preferred_element_type=F32)


def body(
    state_ref, links_ref, lw_ref, mass_ref, flow_ref, src_ref, owner_ref, row_ref, w_ref,
    kxy_ref, vert_ref, pick_ref, place_ref, tvert_ref,
    out_ref, imp_ref,
    ext1, ext2, tail1, tail2, mixm, badv, ab, table, keys, acc, send, recv, imps,
    halo_send, halo_recv, a2a_send, a2a_recv,
):
    comp = lax.axis_index("comp")
    me = lax.axis_index("dom")
    other = 1 - comp
    right = lax.rem(me + 1, OWNERS)
    left = lax.rem(me + OWNERS - 1, OWNERS)
    mid = slice(HW, HW + ROWS)

    barrier = pltpu.get_barrier_semaphore()

    def greet(r, carry):
        pl.semaphore_signal(
            barrier, inc=1, device_id=(other, lax.rem(me + r, OWNERS)), device_id_type=MESH
        )
        return carry

    for side in (left, right):
        pl.semaphore_signal(barrier, inc=1, device_id=(comp, side), device_id_type=MESH)
    lax.fori_loop(0, OWNERS, greet, 0)

    def halo(ext, number):
        copies = []
        for side, src, dst, k in (
            (right, slice(ROWS, ROWS + HW), slice(0, HW), 0),
            (left, slice(HW, 2 * HW), slice(HW + ROWS, 2 * HW + ROWS), 1),
        ):
            copies.append(
                pltpu.make_async_remote_copy(
                    src_ref=ext.at[:, src],
                    dst_ref=ext.at[:, dst],
                    send_sem=halo_send.at[number, k],
                    recv_sem=halo_recv.at[number, k],
                    device_id=(comp, side),
                    device_id_type=MESH,
                )
            )
        return copies

    def advance(x, j):
        return (x.astype(F32) + dot(x, badv[j])).astype(BF)

    mass = mass_ref[...]
    total = jnp.sum(lw_ref[...], axis=0, keepdims=True)

    @pl.when(comp == 0)
    def _():
        inv = 1.0 / (mass + total)
        ab[0:1, :] = mass * inv
        ab[1:2, :] = inv
        for j in range(NB):
            cols = slice(j * BLK, (j + 1) * BLK)
            badv[j] = (
                kxy_ref[0].astype(F32) * flow_ref[0:1, cols] + kxy_ref[1].astype(F32) * flow_ref[1:2, cols]
            ).astype(BF)
        for j in range(NB):
            cols = slice(j * BLK, (j + 1) * BLK)
            ext1[:, HW + j * BLK : HW + (j + 1) * BLK] = advance(state_ref[:, cols], j)

    @pl.when(comp == 1)
    def _():
        half = 0.5 / mass
        ab[0:1, :] = 1.0 - half * total
        ab[1:2, :] = half
        ab[2:3, :] = 0.25 * flow_ref[0:1, :] * flow_ref[0:1, :]
        ext1[:, mid] = state_ref[...]

    pl.semaphore_wait(barrier, OWNERS + 2)
    deep1 = halo(ext1, 0)
    for copy in deep1:
        copy.start()

    for ch in range(CH):
        line = state_ref[ch * LEV : ch * LEV + 1, :].astype(F32)
        for hi in range(8):
            table[ch * 8 + hi : ch * 8 + hi + 1, :] = line[:, hi * 128 : (hi + 1) * 128]
    source = src_ref[...]
    target = row_ref[...]
    relative = jnp.bitwise_and(owner_ref[...] - me + OWNERS, OWNERS - 1)
    first = relative * 8 + lax.shift_right_logical(target, 7)
    keys[0] = jnp.bitwise_and(source, 127).astype(F32)
    keys[1] = lax.shift_right_logical(source, 7).astype(F32)
    keys[2] = jnp.bitwise_and(target, 127).astype(F32)
    keys[3] = first.astype(F32)
    keys[4] = (first - 256).astype(F32)
    sub = lax.broadcasted_iota(jnp.int32, (8, 16, SLAB), 0) * 16 + lax.broadcasted_iota(jnp.int32, (8, 16, SLAB), 1)
    lanes = sub.astype(F32).astype(BF)
    upper = (sub + 128).astype(F32).astype(BF)
    high = lax.broadcasted_iota(jnp.int32, (8, SLAB), 0).astype(F32)
    exported = table[...].astype(BF)
    one, zero = jnp.asarray(1.0, BF), jnp.asarray(0.0, BF)
    chunks = SLAB // 128

    def row_of(which, i):
        return jnp.concatenate([keys[which, pl.ds(i * chunks + k, 1), :] for k in range(chunks)], axis=1)

    def wide(x):
        return jnp.broadcast_to(x, (16, SLAB)).astype(BF)[None]

    def remap(i, carry):
        hot = jnp.where(lanes == wide(row_of(0, i)), one, zero).reshape(128, SLAB)
        found = dot(exported, hot)
        chosen = high == row_of(1, i)
        weight = jnp.concatenate([w_ref[pl.ds(i * chunks + k, 1), :] for k in range(chunks)], axis=1)
        low = lanes == wide(row_of(2, i))
        rows = []
        for ch in range(CH):
            value = jnp.sum(jnp.where(chosen, found[ch * 8 : ch * 8 + 8], 0.0), axis=0, keepdims=True) * weight
            rows.append(jnp.where(low, wide(value), zero).reshape(128, SLAB))
        values = jnp.concatenate(rows, axis=0)
        ka, kb = wide(row_of(3, i)), wide(row_of(4, i))
        spots = jnp.concatenate(
            [
                jnp.where(part == key, one, zero).reshape(128, SLAB)
                for key in (ka, kb)
                for part in (lanes, upper)
            ],
            axis=0,
        )
        acc[...] += dot_t(spots, values)
        return carry

    acc[...] = jnp.zeros_like(acc)
    lax.fori_loop(0, ENT // SLAB, remap, 0)
    for pair in range(2):
        parts = [acc[:, c * 128 : (c + 1) * 128].reshape(OWNERS, 8, 128) for c in (2 * pair, 2 * pair + 1)]
        send[:, pair * 16 : pair * 16 + 16, :] = jnp.concatenate(parts, axis=1).astype(BF)

    def post(r, carry):
        pltpu.make_async_remote_copy(
            src_ref=send.at[r],
            dst_ref=recv.at[r],
            send_sem=a2a_send,
            recv_sem=a2a_recv,
            device_id=(other, lax.rem(me + r, OWNERS)),
            device_id_type=MESH,
        ).start()
        return carry

    lax.fori_loop(0, OWNERS, post, 0)

    def build(slots):
        base = (
            lax.broadcasted_iota(jnp.int32, (128, BLK), 0).astype(F32).astype(BF).reshape(8, 16, BLK)
        )
        for j in range(NB):
            cols = slice(j * BLK, (j + 1) * BLK)
            place = links_ref[:, cols] + lax.broadcasted_iota(jnp.int32, (8, BLK), 1) + HW
            weights = [
                jnp.broadcast_to(lw_ref[s : s + 1, cols], (16, BLK)).astype(BF)[None] for s in range(slots)
            ]

            def piece(k, carry):
                key = (place - k * 128).astype(F32)
                total = jnp.zeros((8, 16, BLK), BF)
                for s in range(slots):
                    spot = jnp.broadcast_to(key[s : s + 1], (16, BLK)).astype(BF)[None]
                    total = total + jnp.where(base == spot, weights[s], zero)
                mixm[j, pl.ds(pl.multiple_of(k * 128, 128), 128), :] = total.reshape(128, BLK)
                return carry

            lax.fori_loop(0, SPAN // 128, piece, 0)

    pl.when(comp == 0)(lambda: build(3))
    pl.when(comp == 1)(lambda: build(7))

    def settled(ext, j, vmat):
        cols = slice(j * BLK, (j + 1) * BLK)
        linked = dot(ext[:, j * BLK : j * BLK + SPAN], mixm[j])
        own = ext[:, HW + j * BLK : HW + (j + 1) * BLK]
        value = ab[0:1, cols] * own.astype(F32) + ab[1:2, cols] * linked
        if vmat is not None:
            value = value + ab[2:3, cols] * dot(vmat, own)
        return value

    for copy in deep1:
        copy.wait()

    @pl.when(comp == 0)
    def _():
        for j in range(NB):
            ext2[:, HW + j * BLK : HW + (j + 1) * BLK] = advance(settled(ext1, j, None).astype(BF), j)

    @pl.when(comp == 1)
    def _():
        for j in range(NB):
            ext2[:, HW + j * BLK : HW + (j + 1) * BLK] = settled(ext1, j, vert_ref[...]).astype(BF)

    deep2 = halo(ext2, 1)
    for copy in deep2:
        copy.start()

    whole = pltpu.make_async_remote_copy(
        src_ref=send, dst_ref=recv, send_sem=a2a_send, recv_sem=a2a_recv,
        device_id=(other, me), device_id_type=MESH,
    )
    whole.wait_recv()
    summed = jnp.sum(recv[...].astype(F32), axis=0)
    imps[...] = jnp.zeros_like(imps)
    for ch in range(CH):
        for hi in range(8):
            imps[ch : ch + 1, hi * 128 : (hi + 1) * 128] = summed[ch * 8 + hi : ch * 8 + hi + 1, :]
    imp_ref[...] = imps[0:CH, :]
    top = lax.broadcasted_iota(jnp.int32, (TAIL, BLK), 0)

    def forced(j):
        cols = slice(j * BLK, (j + 1) * BLK)
        base = dot(pick_ref[...], state_ref[:, cols])
        return (base + jnp.where(top < CH, 0.5, 0.0) * (imps[:, cols] - base)).astype(BF)

    @pl.when(comp == 0)
    def _():
        for j in range(NB):
            tail1[:, HW + j * BLK : HW + (j + 1) * BLK] = advance(forced(j), j)

    @pl.when(comp == 1)
    def _():
        for j in range(NB):
            tail1[:, HW + j * BLK : HW + (j + 1) * BLK] = forced(j)

    shallow1 = halo(tail1, 2)
    for copy in shallow1:
        copy.start()

    for copy in deep2:
        copy.wait()

    @pl.when(comp == 0)
    def _():
        for j in range(NB):
            out_ref[:, j * BLK : (j + 1) * BLK] = settled(ext2, j, None).astype(BF)

    @pl.when(comp == 1)
    def _():
        for j in range(NB):
            out_ref[:, j * BLK : (j + 1) * BLK] = settled(ext2, j, vert_ref[...]).astype(BF)

    for copy in shallow1:
        copy.wait()

    @pl.when(comp == 0)
    def _():
        for j in range(NB):
            tail2[:, HW + j * BLK : HW + (j + 1) * BLK] = advance(settled(tail1, j, None).astype(BF), j)

    @pl.when(comp == 1)
    def _():
        for j in range(NB):
            own = slice(HW + j * BLK, HW + (j + 1) * BLK)
            deep = dot(pick_ref[...], ext2[:, own])
            tail2[:, own] = jnp.where(top < 12, settled(tail1, j, tvert_ref[...]), deep).astype(BF)

    shallow2 = halo(tail2, 3)
    for copy in shallow2:
        copy.start()
    for copy in shallow2:
        copy.wait()

    def finish(vmat):
        for j in range(NB):
            cols = slice(j * BLK, (j + 1) * BLK)
            last = settled(tail2, j, vmat).astype(BF)
            for ch in range(CH):
                rows = slice(ch * LEV, ch * LEV + TAIL)
                spread = dot(place_ref[ch * TAIL : (ch + 1) * TAIL, :], last)
                out_ref[rows, cols] = jnp.where(top < 3, spread, out_ref[rows, cols].astype(F32)).astype(BF)

    pl.when(comp == 0)(lambda: finish(None))
    pl.when(comp == 1)(lambda: finish(tvert_ref[...]))
    whole.wait_send()


def shards(state, links, link_weight, point_mass, flow, ov_src, ov_owner, ov_row, ov_weight):
    vm = pl.BlockSpec(memory_space=pltpu.VMEM)
    wide = 2 * HW + ROWS
    new, imported = pl.pallas_call(
        body,
        out_shape=(
            jax.ShapeDtypeStruct((CH * LEV, ROWS), BF),
            jax.ShapeDtypeStruct((CH, ROWS), F32),
        ),
        in_specs=[vm] * 14,
        out_specs=(vm, vm),
        scratch_shapes=[
            pltpu.VMEM((CH * LEV, wide), BF),
            pltpu.VMEM((CH * LEV, wide), BF),
            pltpu.VMEM((TAIL, wide), BF),
            pltpu.VMEM((TAIL, wide), BF),
            pltpu.VMEM((NB, SPAN, BLK), BF),
            pltpu.VMEM((NB, BLK, BLK), BF),
            pltpu.VMEM((8, ROWS), F32),
            pltpu.VMEM((CH * 8, 128), F32),
            pltpu.VMEM((5, ENT // 128, 128), F32),
            pltpu.VMEM((OWNERS * 8, CH * 128), F32),
            pltpu.VMEM((OWNERS, CH * 8, 128), BF),
            pltpu.VMEM((OWNERS, CH * 8, 128), BF),
            pltpu.VMEM((TAIL, ROWS), F32),
            pltpu.SemaphoreType.DMA((4, 2)),
            pltpu.SemaphoreType.DMA((4, 2)),
            pltpu.SemaphoreType.DMA,
            pltpu.SemaphoreType.DMA,
        ],
        compiler_params=pltpu.CompilerParams(
            collective_id=0, has_side_effects=True, vmem_limit_bytes=48 * 1024 * 1024
        ),
        name="coupled",
    )(
        state.reshape(CH * LEV, ROWS),
        links,
        link_weight,
        point_mass.reshape(1, ROWS),
        flow,
        ov_src.reshape(ENT // 128, 128),
        ov_owner.reshape(ENT // 128, 128),
        ov_row.reshape(ENT // 128, 128),
        ov_weight.reshape(ENT // 128, 128),
        *constants(),
    )
    return new.reshape(CH, LEV, ROWS), imported


def solution(mesh):
    in_specs = (
        P(None, None, ("comp", "dom")),
        P(None, ("comp", "dom")),
        P(None, ("comp", "dom")),
        P(("comp", "dom")),
        P(None, ("comp", "dom")),
        P(("comp", "dom")),
        P(("comp", "dom"), None),
        P(("comp", "dom")),
        P(("comp", "dom")),
    )
    out_specs = (P(None, None, ("comp", "dom")), P(None, ("comp", "dom")))
    return jax.shard_map(shards, mesh=mesh, in_specs=in_specs, out_specs=out_specs, check_vma=False)
```

```python
import math

import jax
import jax.numpy as jnp
import numpy as np
from jax import lax
from jax.experimental import pallas as pl
from jax.experimental.pallas import tpu as pltpu
from jax.sharding import PartitionSpec as P

CH = 4
LEV = 64
ROWS = 1024
HW = 512
BLK = 256
NB = ROWS // BLK
SPAN = BLK + 2 * HW
OWNERS = 64
PLANE = 16
ENT = 8192
SLAB = 1024
TAIL = 16
MESH = pl.DeviceIdType.MESH
BF = jnp.bfloat16
F32 = jnp.float32


def derivative():
    nodes = np.array([-1.0, -1.0 / math.sqrt(5.0), 1.0 / math.sqrt(5.0), 1.0])
    weights = np.ones(4)
    for column in range(4):
        for middle in range(4):
            if middle != column:
                weights[column] = weights[column] / (nodes[column] - nodes[middle])
    table = np.zeros((4, 4))
    for target in range(4):
        for column in range(4):
            if column != target:
                table[target, column] = weights[column] / weights[target] / (nodes[target] - nodes[column])
        table[target, target] = -np.sum(table[target])
    return table


def element_table():
    d = derivative()
    along_x = np.kron(np.eye(4), d)
    along_y = np.kron(d, np.eye(4))
    return jnp.asarray(-0.04 * np.concatenate([np.tile(along_x.T, (1, 16)), np.tile(along_y.T, (1, 16))]), F32)


def index(shape, dim):
    return lax.broadcasted_iota(jnp.int32, shape, dim)


def ones_where(mask):
    return jnp.where(mask, 1.0, 0.0)


def vertical(rows):
    r, c = index((rows, rows), 0), index((rows, rows), 1)
    level = r & (LEV - 1)
    up = ones_where((c == r + 1) & (level < LEV - 1))
    down = ones_where((c == r - 1) & (level > 0))
    here = ones_where(c == r) * (ones_where(level < LEV - 1) + ones_where(level > 0))
    return (up + down - here).astype(BF)


def dot(a, b):
    return lax.dot_general(a, b, (((1,), (0,)), ((), ())), preferred_element_type=F32)


def dot_t(a, b):
    return lax.dot_general(a, b, (((1,), (1,)), ((), ())), preferred_element_type=F32)


def body(
    state_in, links_in, lw_in, mass_in, flow_in, src_in, owner_in, row_in, w_in, kxy_in,
    out_ref, imp_ref,
    links_ref, lw_ref, mass_ref, flow_ref, src_ref, owner_ref, row_ref, w_ref, kxy_ref,
    load_sem, vert_ref, meta, wind, ext1, ext2, mixm, badv, ab,
    table, keys, values_ref, send, recv, row_send, row_recv, before, after, sums, imps,
    halo_send, halo_recv, plane_send, plane_recv, line_send, line_recv, end_send, end_recv,
):
    comp = lax.axis_index("comp")
    me = lax.axis_index("dom")
    other = 1 - comp
    mz, my, mx = me // 16, lax.rem(me // 4, 4), lax.rem(me, 4)
    row = me - mx
    right = lax.rem(me + 1, OWNERS)
    left = lax.rem(me + OWNERS - 1, OWNERS)
    next_row = lax.rem(row + 4, OWNERS)
    previous_row = lax.rem(row + OWNERS - 4, OWNERS)

    def plane(q, sign):
        dz, dy = q // 4, lax.rem(q, 4)
        return lax.rem(mz + sign * dz + 4, 4) * 16 + lax.rem(my + sign * dy + 4, 4) * 4 + mx

    mid = slice(ROWS, 2 * ROWS)

    pairs = (
        (state_in, ext1.at[:, mid]), (src_in, src_ref), (row_in, row_ref), (owner_in, owner_ref), (w_in, w_ref),
        (flow_in, flow_ref), (mass_in, mass_ref), (lw_in, lw_ref), (links_in, links_ref), (kxy_in, kxy_ref),
    )
    loads = [pltpu.make_async_copy(a, b, load_sem.at[i]) for i, (a, b) in enumerate(pairs)]
    for copy in loads:
        copy.start()
    barrier = pltpu.get_barrier_semaphore()

    def greet(q, carry):
        pl.semaphore_signal(barrier, inc=1, device_id=(other, plane(q, -1)), device_id_type=MESH)
        return carry

    for side in (left, right):
        pl.semaphore_signal(barrier, inc=1, device_id=(comp, side), device_id_type=MESH)
    for k in range(1, 4):
        pl.semaphore_signal(barrier, inc=1, device_id=(comp, row + lax.rem(mx + k, 4)), device_id_type=MESH)

    @pl.when(mx == 0)
    def _():
        for k in range(4):
            pl.semaphore_signal(barrier, inc=1, device_id=(comp, previous_row + k), device_id_type=MESH)

    @pl.when(mx == 3)
    def _():
        for k in range(4):
            pl.semaphore_signal(barrier, inc=1, device_id=(comp, next_row + k), device_id_type=MESH)

    lax.fori_loop(0, PLANE, greet, 0)

    def halo(ext, width, number):
        own = ext.shape[1] - 2 * width
        copies = []
        for side, src, dst, k in (
            (right, slice(own, own + width), slice(0, width), 0),
            (left, slice(width, 2 * width), slice(own + width, own + 2 * width), 1),
        ):
            copies.append(
                pltpu.make_async_remote_copy(
                    src_ref=ext.at[:, src],
                    dst_ref=ext.at[:, dst],
                    send_sem=halo_send.at[number, k],
                    recv_sem=halo_recv.at[number, k],
                    device_id=(comp, side),
                    device_id_type=MESH,
                )
            )
        return copies

    for copy in loads:
        copy.wait()

    meta[0:8, HW : HW + ROWS] = links_ref[...].astype(F32)
    meta[8:16, HW : HW + ROWS] = lw_ref[...]
    wind[:, mid] = jnp.concatenate([flow_ref[...], jnp.zeros((6, ROWS), F32)], axis=0)
    meta[16:24, HW : HW + ROWS] = jnp.concatenate(
        [mass_ref[...], flow_ref[...], jnp.zeros((5, ROWS), F32)], axis=0
    )
    element = index((16, BLK), 1) >> 4

    def factors(blocks):
        for b in blocks:
            cols = slice(b * BLK, (b + 1) * BLK)
            total = jnp.sum(meta[8:16, cols], axis=0, keepdims=True)
            mass = meta[16:17, cols]

            @pl.when(comp == 0)
            def _():
                inv = 1.0 / (mass + total)
                ab[0:1, cols] = mass * inv
                ab[1:2, cols] = inv

            @pl.when(comp == 1)
            def _():
                half = 0.5 / mass
                ab[0:1, cols] = 1.0 - half * total
                ab[1:2, cols] = half
                ab[2:3, cols] = 0.25 * meta[17:18, cols] * meta[17:18, cols]

    def slopes(blocks):
        for g in blocks:
            cols = slice(g * BLK, (g + 1) * BLK)
            slope = kxy_ref[0:16, :] * wind[0:1, cols] + kxy_ref[16:32, :] * wind[1:2, cols]
            for p in range(BLK // 16):
                badv[g, p * 16 : p * 16 + 16, :] = jnp.where(element == p, slope, 0.0).astype(BF)

    def combine(blocks):
        for b in blocks:
            cols = slice(b * BLK, (b + 1) * BLK)
            for k in range(SPAN // BLK):
                rows = slice(k * BLK, (k + 1) * BLK)
                part = mixm[b, rows, :]
                value = part.astype(F32) + dot(badv[b + k], part)
                if k == 2:
                    value = value + ab[0:1, cols] * badv[b + 2].astype(F32)
                mixm[b, rows, :] = value.astype(BF)

    own_blocks = range(2, 2 + NB)

    pl.semaphore_wait(barrier, PLANE + 7)
    small_halo = halo(meta, HW, 0) + halo(wind, ROWS, 1)
    deep_halo = [
        pltpu.make_async_remote_copy(
            src_ref=state_in,
            dst_ref=ext1.at[:, dst],
            send_sem=halo_send.at[2, k],
            recv_sem=halo_recv.at[2, k],
            device_id=(comp, side),
            device_id_type=MESH,
        )
        for side, dst, k in ((right, slice(0, ROWS), 0), (left, slice(2 * ROWS, 3 * ROWS), 1))
    ]
    for copy in small_halo + deep_halo:
        copy.start()

    for ch in range(CH):
        line = ext1[ch * LEV : ch * LEV + 1, mid].astype(F32)
        for hi in range(8):
            table[ch * 8 + hi : ch * 8 + hi + 1, :] = line[:, hi * 128 : (hi + 1) * 128]
    source = src_ref[...]
    target = row_ref[...]
    owner = owner_ref[...]
    relative = (
        jnp.bitwise_and(lax.shift_right_logical(owner, 4) - mz + 4, 3) * 16
        + jnp.bitwise_and(lax.shift_right_logical(owner, 2) - my + 4, 3) * 4
        + jnp.bitwise_and(owner, 3)
    )
    first = relative * 8 + lax.shift_right_logical(target, 7)
    keys[0] = jnp.bitwise_and(source, 127).astype(F32)
    keys[1] = lax.shift_right_logical(source, 7).astype(F32)
    keys[2] = jnp.bitwise_and(target, 127).astype(F32)
    keys[3] = first.astype(F32)
    keys[4] = (first - 256).astype(F32)
    sub = index((8, 16, SLAB), 0) * 16 + index((8, 16, SLAB), 1)
    lanes = sub.astype(F32).astype(BF)
    upper = (sub + 128).astype(F32).astype(BF)
    high = index((8, SLAB), 0).astype(F32)
    exported = table[...].astype(BF)
    one, zero = jnp.asarray(1.0, BF), jnp.asarray(0.0, BF)
    chunks = SLAB // 128

    def row_of(which, i):
        return jnp.concatenate([keys[which, pl.ds(i * chunks + k, 1), :] for k in range(chunks)], axis=1)

    def wide(x):
        return jnp.broadcast_to(x, (16, SLAB)).astype(BF)[None]

    def spots(which, i):
        key = wide(row_of(which, i))
        return jnp.concatenate(
            [jnp.where(part == key, one, zero).reshape(128, SLAB) for part in (lanes, upper)], axis=0
        )

    def first_part(i, total):
        hot = jnp.where(lanes == wide(row_of(0, i)), one, zero).reshape(128, SLAB)
        found = dot(exported, hot)
        chosen = high == row_of(1, i)
        weight = jnp.concatenate([w_ref[pl.ds(i * chunks + k, 1), :] for k in range(chunks)], axis=1)
        low = lanes == wide(row_of(2, i))
        rows = []
        for ch in range(CH):
            value = jnp.sum(jnp.where(chosen, found[ch * 8 : ch * 8 + 8], 0.0), axis=0, keepdims=True) * weight
            rows.append(jnp.where(low, wide(value), zero).reshape(128, SLAB))
        values = jnp.concatenate(rows, axis=0)
        values_ref[i] = values
        return total + dot_t(spots(3, i), values)

    def second_part(i, total):
        return total + dot_t(spots(4, i), values_ref[i])

    half_owners = OWNERS // 2

    def pack(part, total):
        for pair in range(2):
            parts = [
                total[:, c * 128 : (c + 1) * 128].reshape(half_owners, 8, 128) for c in (2 * pair, 2 * pair + 1)
            ]
            send[part * half_owners : (part + 1) * half_owners, pair * 16 : pair * 16 + 16, :] = jnp.concatenate(
                parts, axis=1
            ).astype(BF)

    def post(part):
        def one_post(q, carry):
            pltpu.make_async_remote_copy(
                src_ref=send.at[pl.ds(q * 4, 4)],
                dst_ref=recv.at[pl.ds(q * 4, 4)],
                send_sem=plane_send.at[part],
                recv_sem=plane_recv.at[part],
                device_id=(other, plane(q, 1)),
                device_id_type=MESH,
            ).start()
            return carry

        lax.fori_loop(part * PLANE // 2, (part + 1) * PLANE // 2, one_post, 0)

    start = jnp.zeros((256, CH * 128), F32)
    pack(0, lax.fori_loop(0, ENT // SLAB, first_part, start, unroll=True))
    post(0)
    pack(1, lax.fori_loop(0, ENT // SLAB, second_part, start, unroll=True))
    post(1)

    base_iota = index((128, BLK), 0).astype(F32).astype(BF).reshape(8, 16, BLK)

    def build(slots, blocks):
        for b in blocks:
            cols = slice(b * BLK, (b + 1) * BLK)
            place = meta[0:8, cols] + (index((8, BLK), 1) + HW).astype(F32)
            weights = [
                jnp.broadcast_to(meta[8 + s : 9 + s, cols] * ab[1:2, cols], (16, BLK)).astype(BF)[None] for s in range(slots)
            ]

            def piece(k, carry):
                key = place - (k * 128).astype(F32)
                total = jnp.zeros((8, 16, BLK), BF)
                for s in range(slots):
                    spot = jnp.broadcast_to(key[s : s + 1], (16, BLK)).astype(BF)[None]
                    total = total + jnp.where(base_iota == spot, weights[s], zero)
                mixm[b, pl.ds(pl.multiple_of(k * 128, 128), 128), :] = total.reshape(128, BLK)
                return carry

            lax.fori_loop(0, SPAN // 128, piece, 0)

    vert_ref[...] = vertical(CH * LEV)
    factors(own_blocks)

    @pl.when(comp == 0)
    def _():
        slopes(range(NB, 2 * NB))
        build(3, own_blocks)

    pl.when(comp == 1)(lambda: build(7, own_blocks))
    for copy in small_halo:
        copy.wait()
    sides = (0, 1, 6, 7)
    factors(sides)

    @pl.when(comp == 0)
    def _():
        slopes((0, 1, 2, 3, 8, 9, 10, 11))
        build(3, sides)
        combine(range(2 * NB))

    pl.when(comp == 1)(lambda: build(7, sides))

    def settled(window, own, b, vmat):
        cols = slice(b * BLK, (b + 1) * BLK)
        value = ab[0:1, cols] * own.astype(F32) + dot(window, mixm[b])
        if vmat is not None:
            value = value + ab[2:3, cols] * dot(vmat, own)
        return value

    def first_step(ext, b, vmat):
        own = ext[:, HW + b * BLK : HW + (b + 1) * BLK]
        return settled(ext[:, b * BLK : b * BLK + SPAN], own, b, vmat)

    def second_step(ext, j, vmat):
        own = ext[:, HW + j * BLK : HW + (j + 1) * BLK]
        return settled(ext[:, j * BLK : j * BLK + SPAN], own, j + 2, vmat)

    def arrived(part):
        rows = slice(part * half_owners, (part + 1) * half_owners)
        return pltpu.make_async_remote_copy(
            src_ref=send.at[rows], dst_ref=recv.at[rows], send_sem=plane_send.at[part], recv_sem=plane_recv.at[part],
            device_id=(other, me), device_id_type=MESH,
        )

    total = jnp.zeros((4, CH * 8, 128), F32)
    for part in range(2):
        arrived(part).wait_recv()
        rows = slice(part * half_owners, (part + 1) * half_owners)
        total = total + jnp.sum(recv[rows].astype(F32).reshape(PLANE // 2, 4, CH * 8, 128), axis=0)
    row_send[...] = total.astype(BF)
    line = []
    for k in range(1, 4):
        line.append(
            pltpu.make_async_remote_copy(
                src_ref=row_send, dst_ref=row_recv.at[k - 1], send_sem=line_send.at[k - 1], recv_sem=line_recv.at[k - 1],
                device_id=(comp, row + lax.rem(mx + k, 4)), device_id_type=MESH,
            )
        )

    def end(which, slot, target, source, k):
        return pltpu.make_async_remote_copy(
            src_ref=row_send.at[source], dst_ref=which.at[slot], send_sem=end_send.at[k], recv_sem=end_recv.at[k, slot],
            device_id=(comp, target), device_id_type=MESH,
        )

    ends = [end(before, mx, next_row, 3, 0), end(after, mx, previous_row + 3, 0, 1)]
    for copy in ends + line:
        copy.start()

    for copy in deep_halo:
        copy.wait()
    for copy in line:
        copy.wait()
    total = row_send[...].astype(F32)
    for k in range(3):
        total = total + row_recv[k].astype(F32)
    sums[1:5] = total

    @pl.when(mx == 0)
    def _():
        for k in range(4):
            end(before, k, next_row, 3, 0).wait_recv()
        sums[0] = jnp.sum(before[...].astype(F32), axis=0)

    @pl.when(mx == 3)
    def _():
        for k in range(4):
            end(after, k, previous_row + 3, 0, 1).wait_recv()
        sums[5] = jnp.sum(after[...].astype(F32), axis=0)

    for side in range(3):
        block = sums[mx + side]
        for ch in range(CH):
            for hi in range(8):
                cols = slice(side * ROWS + hi * 128, side * ROWS + (hi + 1) * 128)
                imps[ch : ch + 1, cols] = block[ch * 8 + hi : ch * 8 + hi + 1, :]
    imp_ref[...] = imps[0:CH, mid]
    top = index((TAIL, BLK), 0)

    for g in range(3 * NB):
        cols = slice(g * BLK, (g + 1) * BLK)
        for ch in range(CH):
            rows = slice(ch * LEV, ch * LEV + TAIL)
            old = ext1[rows, cols].astype(F32)
            new = old + 0.5 * (imps[ch : ch + 1, cols] - old)
            ext1[rows, cols] = jnp.where(top == 0, new, old).astype(BF)

    def steps(vmat):
        for b in range(2 * NB):
            ext2[:, b * BLK : (b + 1) * BLK] = first_step(ext1, b, vmat).astype(BF)
        for j in range(NB):
            out_ref[:, j * BLK : (j + 1) * BLK] = second_step(ext2, j, vmat).astype(BF)

    pl.when(comp == 0)(lambda: steps(None))
    pl.when(comp == 1)(lambda: steps(vert_ref[...]))
    for copy in ends:
        copy.wait_send()
    arrived(0).wait_send()
    arrived(1).wait_send()


def shards(state, links, link_weight, point_mass, flow, ov_src, ov_owner, ov_row, ov_weight):
    hbm = pl.BlockSpec(memory_space=pl.ANY)
    vm = pl.BlockSpec(memory_space=pltpu.VMEM)
    operands = (
        state.reshape(CH * LEV, ROWS),
        links,
        link_weight,
        point_mass.reshape(1, ROWS),
        flow,
        ov_src.reshape(ENT // 128, 128),
        ov_owner.reshape(ENT // 128, 128),
        ov_row.reshape(ENT // 128, 128),
        ov_weight.reshape(ENT // 128, 128),
        element_table(),
    )
    new, imported = pl.pallas_call(
        body,
        out_shape=(
            jax.ShapeDtypeStruct((CH * LEV, ROWS), BF),
            jax.ShapeDtypeStruct((CH, ROWS), F32),
        ),
        in_specs=[hbm] * 10,
        out_specs=(vm, vm),
        scratch_shapes=[pltpu.VMEM(x.shape, x.dtype) for x in operands[1:]]
        + [
            pltpu.SemaphoreType.DMA((10,)),
            pltpu.VMEM((CH * LEV, CH * LEV), BF),
            pltpu.VMEM((24, 2 * ROWS), F32),
            pltpu.VMEM((8, 3 * ROWS), F32),
            pltpu.VMEM((CH * LEV, 3 * ROWS), BF),
            pltpu.VMEM((CH * LEV, 2 * ROWS), BF),
            pltpu.VMEM((2 * NB, SPAN, BLK), BF),
            pltpu.VMEM((3 * NB, BLK, BLK), BF),
            pltpu.VMEM((8, 2 * ROWS), F32),
            pltpu.VMEM((CH * 8, 128), F32),
            pltpu.VMEM((5, ENT // 128, 128), F32),
            pltpu.VMEM((ENT // SLAB, CH * 128, SLAB), BF),
            pltpu.VMEM((OWNERS, CH * 8, 128), BF),
            pltpu.VMEM((OWNERS, CH * 8, 128), BF),
            pltpu.VMEM((4, CH * 8, 128), BF),
            pltpu.VMEM((3, 4, CH * 8, 128), BF),
            pltpu.VMEM((4, CH * 8, 128), BF),
            pltpu.VMEM((4, CH * 8, 128), BF),
            pltpu.VMEM((6, CH * 8, 128), F32),
            pltpu.VMEM((8, 3 * ROWS), F32),
            pltpu.SemaphoreType.DMA((3, 2)),
            pltpu.SemaphoreType.DMA((3, 2)),
            pltpu.SemaphoreType.DMA((2,)),
            pltpu.SemaphoreType.DMA((2,)),
            pltpu.SemaphoreType.DMA((3,)),
            pltpu.SemaphoreType.DMA((3,)),
            pltpu.SemaphoreType.DMA((2,)),
            pltpu.SemaphoreType.DMA((2, 4)),
        ],
        compiler_params=pltpu.CompilerParams(
            collective_id=0, has_side_effects=True, vmem_limit_bytes=56 * 1024 * 1024
        ),
        name="coupled",
    )(*operands)
    return new.reshape(CH, LEV, ROWS), imported


def solution(mesh):
    in_specs = (
        P(None, None, ("comp", "dom")),
        P(None, ("comp", "dom")),
        P(None, ("comp", "dom")),
        P(("comp", "dom")),
        P(None, ("comp", "dom")),
        P(("comp", "dom")),
        P(("comp", "dom"), None),
        P(("comp", "dom")),
        P(("comp", "dom")),
    )
    out_specs = (P(None, None, ("comp", "dom")), P(None, ("comp", "dom")))
    return jax.shard_map(shards, mesh=mesh, in_specs=in_specs, out_specs=out_specs, check_vma=False)
```

```python
import math

import jax
import jax.numpy as jnp
import numpy as np
from jax import lax
from jax.experimental import pallas as pl
from jax.experimental.pallas import tpu as pltpu
from jax.sharding import PartitionSpec as P

CH = 4
LEV = 64
ROWS = 1024
HW = 512
BLK = 256
NB = ROWS // BLK
SPAN = BLK + 2 * HW
OWNERS = 64
PLANE = 16
ENT = 8192
SLAB = 1024
TAIL = 16
MESH = pl.DeviceIdType.MESH
BF = jnp.bfloat16
F32 = jnp.float32


def derivative():
    nodes = np.array([-1.0, -1.0 / math.sqrt(5.0), 1.0 / math.sqrt(5.0), 1.0])
    weights = np.ones(4)
    for column in range(4):
        for middle in range(4):
            if middle != column:
                weights[column] = weights[column] / (nodes[column] - nodes[middle])
    table = np.zeros((4, 4))
    for target in range(4):
        for column in range(4):
            if column != target:
                table[target, column] = weights[column] / weights[target] / (nodes[target] - nodes[column])
        table[target, target] = -np.sum(table[target])
    return table


def element_table():
    d = derivative()
    along_x = np.kron(np.eye(4), d)
    along_y = np.kron(d, np.eye(4))
    return jnp.asarray(-0.04 * np.concatenate([np.tile(along_x.T, (1, 16)), np.tile(along_y.T, (1, 16))]), F32)


def index(shape, dim):
    return lax.broadcasted_iota(jnp.int32, shape, dim)


def ones_where(mask):
    return jnp.where(mask, 1.0, 0.0)


def vertical(rows):
    r, c = index((rows, rows), 0), index((rows, rows), 1)
    level = r & (LEV - 1)
    up = ones_where((c == r + 1) & (level < LEV - 1))
    down = ones_where((c == r - 1) & (level > 0))
    here = ones_where(c == r) * (ones_where(level < LEV - 1) + ones_where(level > 0))
    return (up + down - here).astype(BF)


def dot(a, b):
    return lax.dot_general(a, b, (((1,), (0,)), ((), ())), preferred_element_type=F32)


def dot_t(a, b):
    return lax.dot_general(a, b, (((1,), (1,)), ((), ())), preferred_element_type=F32)


def body(
    state_in, links_in, lw_in, mass_in, flow_in, src_in, owner_in, row_in, w_in, kxy_in,
    out_ref, imp_ref,
    links_ref, lw_ref, mass_ref, flow_ref, src_ref, owner_ref, row_ref, w_ref, kxy_ref,
    load_sem, vert_ref, meta, wind, ext1, ext2, mixm, badv, ab,
    table, keys, values_ref, send, recv, row_send, row_recv, before, after, sums, imps, relay,
    halo_send, halo_recv, deep_send, deep_recv, relay_recv, forward_send, plane_send, plane_recv, line_send, line_recv, end_send, end_recv,
):
    comp = lax.axis_index("comp")
    me = lax.axis_index("dom")
    other = 1 - comp
    mz, my, mx = me // 16, lax.rem(me // 4, 4), lax.rem(me, 4)
    row = me - mx
    right = lax.rem(me + 1, OWNERS)
    left = lax.rem(me + OWNERS - 1, OWNERS)
    next_row = lax.rem(row + 4, OWNERS)
    previous_row = lax.rem(row + OWNERS - 4, OWNERS)

    def plane(q, sign):
        dz, dy = q // 4, lax.rem(q, 4)
        return lax.rem(mz + sign * dz + 4, 4) * 16 + lax.rem(my + sign * dy + 4, 4) * 4 + mx

    mid = slice(ROWS, 2 * ROWS)

    pairs = (
        (state_in, ext1.at[:, mid]), (src_in, src_ref), (row_in, row_ref), (owner_in, owner_ref), (w_in, w_ref),
        (flow_in, flow_ref), (mass_in, mass_ref), (lw_in, lw_ref), (links_in, links_ref), (kxy_in, kxy_ref),
    )
    loads = [pltpu.make_async_copy(a, b, load_sem.at[i]) for i, (a, b) in enumerate(pairs)]
    for copy in loads:
        copy.start()
    barrier = pltpu.get_barrier_semaphore()

    def greet(q, carry):
        pl.semaphore_signal(barrier, inc=1, device_id=(other, plane(q, -1)), device_id_type=MESH)
        return carry

    for side in (left, right):
        pl.semaphore_signal(barrier, inc=1, device_id=(comp, side), device_id_type=MESH)
    for k in range(1, 4):
        pl.semaphore_signal(barrier, inc=1, device_id=(comp, row + lax.rem(mx + k, 4)), device_id_type=MESH)

    @pl.when(mx == 0)
    def _():
        for k in range(4):
            pl.semaphore_signal(barrier, inc=1, device_id=(comp, previous_row + k), device_id_type=MESH)
        pl.semaphore_signal(barrier, inc=1, device_id=(comp, next_row), device_id_type=MESH)

    @pl.when(mx == 3)
    def _():
        for k in range(4):
            pl.semaphore_signal(barrier, inc=1, device_id=(comp, next_row + k), device_id_type=MESH)
        pl.semaphore_signal(barrier, inc=1, device_id=(comp, previous_row + 3), device_id_type=MESH)

    lax.fori_loop(0, PLANE, greet, 0)

    def halo(ext, width, number):
        own = ext.shape[1] - 2 * width
        copies = []
        for side, src, dst, k in (
            (right, slice(own, own + width), slice(0, width), 0),
            (left, slice(width, 2 * width), slice(own + width, own + 2 * width), 1),
        ):
            copies.append(
                pltpu.make_async_remote_copy(
                    src_ref=ext.at[:, src],
                    dst_ref=ext.at[:, dst],
                    send_sem=halo_send.at[number, k],
                    recv_sem=halo_recv.at[number, k],
                    device_id=(comp, side),
                    device_id_type=MESH,
                )
            )
        return copies

    for copy in loads:
        copy.wait()

    meta[0:8, HW : HW + ROWS] = links_ref[...].astype(F32)
    meta[8:16, HW : HW + ROWS] = lw_ref[...]
    wind[:, mid] = jnp.concatenate([flow_ref[...], jnp.zeros((6, ROWS), F32)], axis=0)
    meta[16:24, HW : HW + ROWS] = jnp.concatenate(
        [mass_ref[...], flow_ref[...], jnp.zeros((5, ROWS), F32)], axis=0
    )
    element = index((16, BLK), 1) >> 4

    def factors(blocks):
        for b in blocks:
            cols = slice(b * BLK, (b + 1) * BLK)
            total = jnp.sum(meta[8:16, cols], axis=0, keepdims=True)
            mass = meta[16:17, cols]

            @pl.when(comp == 0)
            def _():
                inv = 1.0 / (mass + total)
                ab[0:1, cols] = mass * inv
                ab[1:2, cols] = inv

            @pl.when(comp == 1)
            def _():
                half = 0.5 / mass
                ab[0:1, cols] = 1.0 - half * total
                ab[1:2, cols] = half
                ab[2:3, cols] = 0.25 * meta[17:18, cols] * meta[17:18, cols]

    def slopes(blocks):
        for g in blocks:
            cols = slice(g * BLK, (g + 1) * BLK)
            slope = kxy_ref[0:16, :] * wind[0:1, cols] + kxy_ref[16:32, :] * wind[1:2, cols]
            for p in range(BLK // 16):
                badv[g, p * 16 : p * 16 + 16, :] = jnp.where(element == p, slope, 0.0).astype(BF)

    def combine(blocks):
        for b in blocks:
            cols = slice(b * BLK, (b + 1) * BLK)
            for k in range(SPAN // BLK):
                rows = slice(k * BLK, (k + 1) * BLK)
                part = mixm[b, rows, :]
                value = part.astype(F32) + dot(badv[b + k], part)
                if k == 2:
                    value = value + ab[0:1, cols] * badv[b + 2].astype(F32)
                mixm[b, rows, :] = value.astype(BF)

    own_blocks = range(2, 2 + NB)

    at_start, at_end = mx == 0, mx == 3
    pl.semaphore_wait(barrier, jnp.where(at_start | at_end, PLANE + 8, PLANE + 7))
    small_halo = halo(meta, HW, 0) + halo(wind, ROWS, 1)
    half_rows = CH * LEV // 2
    sides = ((right, slice(0, ROWS)), (left, slice(2 * ROWS, 3 * ROWS)))

    def deep(half, k):
        rows = slice(half * half_rows, (half + 1) * half_rows)
        side, dst = sides[k]
        return pltpu.make_async_remote_copy(
            src_ref=state_in.at[rows], dst_ref=ext1.at[rows, dst],
            send_sem=deep_send.at[half, k], recv_sem=deep_recv.at[half, k],
            device_id=(comp, side), device_id_type=MESH,
        )

    def to_relay(k):
        return pltpu.make_async_remote_copy(
            src_ref=state_in.at[half_rows : 2 * half_rows], dst_ref=relay,
            send_sem=deep_send.at[1, k], recv_sem=relay_recv.at[k],
            device_id=(comp, next_row + 3 if k == 0 else previous_row), device_id_type=MESH,
        )

    def from_relay(k):
        return pltpu.make_async_remote_copy(
            src_ref=relay, dst_ref=ext1.at[half_rows : 2 * half_rows, sides[k][1]],
            send_sem=forward_send, recv_sem=deep_recv.at[1, k],
            device_id=(comp, row if k == 0 else row + 3), device_id_type=MESH,
        )

    for copy in small_halo:
        copy.start()
    for k, edge in ((0, at_end), (1, at_start)):
        pl.when(edge)(to_relay(k).start)
    for k in range(2):
        deep(0, k).start()
    for k, edge in ((0, at_end), (1, at_start)):
        pl.when(jnp.logical_not(edge))(deep(1, k).start)

    for ch in range(CH):
        line = ext1[ch * LEV : ch * LEV + 1, mid].astype(F32)
        for hi in range(8):
            table[ch * 8 + hi : ch * 8 + hi + 1, :] = line[:, hi * 128 : (hi + 1) * 128]
    source = src_ref[...]
    target = row_ref[...]
    owner = owner_ref[...]
    relative = (
        jnp.bitwise_and(lax.shift_right_logical(owner, 4) - mz + 4, 3) * 16
        + jnp.bitwise_and(lax.shift_right_logical(owner, 2) - my + 4, 3) * 4
        + jnp.bitwise_and(owner, 3)
    )
    first = relative * 8 + lax.shift_right_logical(target, 7)
    keys[0] = jnp.bitwise_and(source, 127).astype(F32)
    keys[1] = lax.shift_right_logical(source, 7).astype(F32)
    keys[2] = jnp.bitwise_and(target, 127).astype(F32)
    keys[3] = first.astype(F32)
    keys[4] = (first - 256).astype(F32)
    sub = index((8, 16, SLAB), 0) * 16 + index((8, 16, SLAB), 1)
    lanes = sub.astype(F32).astype(BF)
    upper = (sub + 128).astype(F32).astype(BF)
    high = index((8, SLAB), 0).astype(F32)
    exported = table[...].astype(BF)
    one, zero = jnp.asarray(1.0, BF), jnp.asarray(0.0, BF)
    chunks = SLAB // 128

    def row_of(which, i):
        return jnp.concatenate([keys[which, pl.ds(i * chunks + k, 1), :] for k in range(chunks)], axis=1)

    def wide(x):
        return jnp.broadcast_to(x, (16, SLAB)).astype(BF)[None]

    def spots(which, i):
        key = wide(row_of(which, i))
        return jnp.concatenate(
            [jnp.where(part == key, one, zero).reshape(128, SLAB) for part in (lanes, upper)], axis=0
        )

    def first_part(i, total):
        hot = jnp.where(lanes == wide(row_of(0, i)), one, zero).reshape(128, SLAB)
        found = dot(exported, hot)
        chosen = high == row_of(1, i)
        weight = jnp.concatenate([w_ref[pl.ds(i * chunks + k, 1), :] for k in range(chunks)], axis=1)
        low = lanes == wide(row_of(2, i))
        rows = []
        for ch in range(CH):
            value = jnp.sum(jnp.where(chosen, found[ch * 8 : ch * 8 + 8], 0.0), axis=0, keepdims=True) * weight
            rows.append(jnp.where(low, wide(value), zero).reshape(128, SLAB))
        values = jnp.concatenate(rows, axis=0)
        values_ref[i] = values
        return total + dot_t(spots(3, i), values)

    def second_part(i, total):
        return total + dot_t(spots(4, i), values_ref[i])

    half_owners = OWNERS // 2

    def pack(part, total):
        for pair in range(2):
            parts = [
                total[:, c * 128 : (c + 1) * 128].reshape(half_owners, 8, 128) for c in (2 * pair, 2 * pair + 1)
            ]
            send[part * half_owners : (part + 1) * half_owners, pair * 16 : pair * 16 + 16, :] = jnp.concatenate(
                parts, axis=1
            ).astype(BF)

    def post(part):
        def one_post(q, carry):
            pltpu.make_async_remote_copy(
                src_ref=send.at[pl.ds(q * 4, 4)],
                dst_ref=recv.at[pl.ds(q * 4, 4)],
                send_sem=plane_send.at[part],
                recv_sem=plane_recv.at[part],
                device_id=(other, plane(q, 1)),
                device_id_type=MESH,
            ).start()
            return carry

        lax.fori_loop(part * PLANE // 2, (part + 1) * PLANE // 2, one_post, 0)

    start = jnp.zeros((256, CH * 128), F32)
    pack(0, lax.fori_loop(0, ENT // SLAB, first_part, start, unroll=True))
    post(0)
    pack(1, lax.fori_loop(0, ENT // SLAB, second_part, start, unroll=True))
    post(1)

    base_iota = index((128, BLK), 0).astype(F32).astype(BF).reshape(8, 16, BLK)

    def build(slots, blocks):
        for b in blocks:
            cols = slice(b * BLK, (b + 1) * BLK)
            place = meta[0:8, cols] + (index((8, BLK), 1) + HW).astype(F32)
            weights = [
                jnp.broadcast_to(meta[8 + s : 9 + s, cols] * ab[1:2, cols], (16, BLK)).astype(BF)[None] for s in range(slots)
            ]

            def piece(k, carry):
                key = place - (k * 128).astype(F32)
                total = jnp.zeros((8, 16, BLK), BF)
                for s in range(slots):
                    spot = jnp.broadcast_to(key[s : s + 1], (16, BLK)).astype(BF)[None]
                    total = total + jnp.where(base_iota == spot, weights[s], zero)
                mixm[b, pl.ds(pl.multiple_of(k * 128, 128), 128), :] = total.reshape(128, BLK)
                return carry

            lax.fori_loop(0, SPAN // 128, piece, 0)

    vert_ref[...] = vertical(CH * LEV)
    factors(own_blocks)

    @pl.when(comp == 0)
    def _():
        slopes(range(NB, 2 * NB))
        build(3, own_blocks)

    pl.when(comp == 1)(lambda: build(7, own_blocks))
    for k, edge in ((0, at_end), (1, at_start)):

        @pl.when(edge)
        def _():
            to_relay(k).wait_recv()
            from_relay(k).start()

    for copy in small_halo:
        copy.wait()
    outer = (0, 1, 6, 7)
    factors(outer)

    @pl.when(comp == 0)
    def _():
        slopes((0, 1, 2, 3, 8, 9, 10, 11))
        build(3, outer)
        combine(range(2 * NB))

    pl.when(comp == 1)(lambda: build(7, outer))

    def settled(window, own, b, vmat):
        cols = slice(b * BLK, (b + 1) * BLK)
        value = ab[0:1, cols] * own.astype(F32) + dot(window, mixm[b])
        if vmat is not None:
            value = value + ab[2:3, cols] * dot(vmat, own)
        return value

    def first_step(ext, b, vmat):
        own = ext[:, HW + b * BLK : HW + (b + 1) * BLK]
        return settled(ext[:, b * BLK : b * BLK + SPAN], own, b, vmat)

    def second_step(ext, j, vmat):
        own = ext[:, HW + j * BLK : HW + (j + 1) * BLK]
        return settled(ext[:, j * BLK : j * BLK + SPAN], own, j + 2, vmat)

    def arrived(part):
        rows = slice(part * half_owners, (part + 1) * half_owners)
        return pltpu.make_async_remote_copy(
            src_ref=send.at[rows], dst_ref=recv.at[rows], send_sem=plane_send.at[part], recv_sem=plane_recv.at[part],
            device_id=(other, me), device_id_type=MESH,
        )

    total = jnp.zeros((4, CH * 8, 128), F32)
    for part in range(2):
        arrived(part).wait_recv()
        rows = slice(part * half_owners, (part + 1) * half_owners)
        total = total + jnp.sum(recv[rows].astype(F32).reshape(PLANE // 2, 4, CH * 8, 128), axis=0)
    row_send[...] = total.astype(BF)
    line = []
    for k in range(1, 4):
        line.append(
            pltpu.make_async_remote_copy(
                src_ref=row_send, dst_ref=row_recv.at[k - 1], send_sem=line_send.at[k - 1], recv_sem=line_recv.at[k - 1],
                device_id=(comp, row + lax.rem(mx + k, 4)), device_id_type=MESH,
            )
        )

    def end(which, slot, target, source, k):
        return pltpu.make_async_remote_copy(
            src_ref=row_send.at[source], dst_ref=which.at[slot], send_sem=end_send.at[k], recv_sem=end_recv.at[k, slot],
            device_id=(comp, target), device_id_type=MESH,
        )

    ends = [end(before, mx, next_row, 3, 0), end(after, mx, previous_row + 3, 0, 1)]
    for copy in ends + line:
        copy.start()

    for half in range(2):
        for k in range(2):
            deep(half, k).wait()
    for copy in line:
        copy.wait()
    total = row_send[...].astype(F32)
    for k in range(3):
        total = total + row_recv[k].astype(F32)
    sums[1:5] = total

    @pl.when(mx == 0)
    def _():
        for k in range(4):
            end(before, k, next_row, 3, 0).wait_recv()
        sums[0] = jnp.sum(before[...].astype(F32), axis=0)

    @pl.when(mx == 3)
    def _():
        for k in range(4):
            end(after, k, previous_row + 3, 0, 1).wait_recv()
        sums[5] = jnp.sum(after[...].astype(F32), axis=0)

    for side in range(3):
        block = sums[mx + side]
        for ch in range(CH):
            for hi in range(8):
                cols = slice(side * ROWS + hi * 128, side * ROWS + (hi + 1) * 128)
                imps[ch : ch + 1, cols] = block[ch * 8 + hi : ch * 8 + hi + 1, :]
    imp_ref[...] = imps[0:CH, mid]
    top = index((TAIL, BLK), 0)

    for g in range(3 * NB):
        cols = slice(g * BLK, (g + 1) * BLK)
        for ch in range(CH):
            rows = slice(ch * LEV, ch * LEV + TAIL)
            old = ext1[rows, cols].astype(F32)
            new = old + 0.5 * (imps[ch : ch + 1, cols] - old)
            ext1[rows, cols] = jnp.where(top == 0, new, old).astype(BF)

    def steps(vmat):
        for b in range(2 * NB):
            ext2[:, b * BLK : (b + 1) * BLK] = first_step(ext1, b, vmat).astype(BF)
        for j in range(NB):
            out_ref[:, j * BLK : (j + 1) * BLK] = second_step(ext2, j, vmat).astype(BF)

    pl.when(comp == 0)(lambda: steps(None))
    pl.when(comp == 1)(lambda: steps(vert_ref[...]))
    pl.when(at_end)(from_relay(0).wait_send)
    pl.when(at_start)(from_relay(1).wait_send)
    for copy in ends:
        copy.wait_send()
    arrived(0).wait_send()
    arrived(1).wait_send()


def shards(state, links, link_weight, point_mass, flow, ov_src, ov_owner, ov_row, ov_weight):
    hbm = pl.BlockSpec(memory_space=pl.ANY)
    vm = pl.BlockSpec(memory_space=pltpu.VMEM)
    operands = (
        state.reshape(CH * LEV, ROWS),
        links,
        link_weight,
        point_mass.reshape(1, ROWS),
        flow,
        ov_src.reshape(ENT // 128, 128),
        ov_owner.reshape(ENT // 128, 128),
        ov_row.reshape(ENT // 128, 128),
        ov_weight.reshape(ENT // 128, 128),
        element_table(),
    )
    new, imported = pl.pallas_call(
        body,
        out_shape=(
            jax.ShapeDtypeStruct((CH * LEV, ROWS), BF),
            jax.ShapeDtypeStruct((CH, ROWS), F32),
        ),
        in_specs=[hbm] * 10,
        out_specs=(vm, vm),
        scratch_shapes=[pltpu.VMEM(x.shape, x.dtype) for x in operands[1:]]
        + [
            pltpu.SemaphoreType.DMA((10,)),
            pltpu.VMEM((CH * LEV, CH * LEV), BF),
            pltpu.VMEM((24, 2 * ROWS), F32),
            pltpu.VMEM((8, 3 * ROWS), F32),
            pltpu.VMEM((CH * LEV, 3 * ROWS), BF),
            pltpu.VMEM((CH * LEV, 2 * ROWS), BF),
            pltpu.VMEM((2 * NB, SPAN, BLK), BF),
            pltpu.VMEM((3 * NB, BLK, BLK), BF),
            pltpu.VMEM((8, 2 * ROWS), F32),
            pltpu.VMEM((CH * 8, 128), F32),
            pltpu.VMEM((5, ENT // 128, 128), F32),
            pltpu.VMEM((ENT // SLAB, CH * 128, SLAB), BF),
            pltpu.VMEM((OWNERS, CH * 8, 128), BF),
            pltpu.VMEM((OWNERS, CH * 8, 128), BF),
            pltpu.VMEM((4, CH * 8, 128), BF),
            pltpu.VMEM((3, 4, CH * 8, 128), BF),
            pltpu.VMEM((4, CH * 8, 128), BF),
            pltpu.VMEM((4, CH * 8, 128), BF),
            pltpu.VMEM((6, CH * 8, 128), F32),
            pltpu.VMEM((8, 3 * ROWS), F32),
            pltpu.VMEM((CH * LEV // 2, ROWS), BF),
            pltpu.SemaphoreType.DMA((2, 2)),
            pltpu.SemaphoreType.DMA((2, 2)),
            pltpu.SemaphoreType.DMA((2, 2)),
            pltpu.SemaphoreType.DMA((2, 2)),
            pltpu.SemaphoreType.DMA((2,)),
            pltpu.SemaphoreType.DMA,
            pltpu.SemaphoreType.DMA((2,)),
            pltpu.SemaphoreType.DMA((2,)),
            pltpu.SemaphoreType.DMA((3,)),
            pltpu.SemaphoreType.DMA((3,)),
            pltpu.SemaphoreType.DMA((2,)),
            pltpu.SemaphoreType.DMA((2, 4)),
        ],
        compiler_params=pltpu.CompilerParams(
            collective_id=0, has_side_effects=True, vmem_limit_bytes=56 * 1024 * 1024
        ),
        name="coupled",
    )(*operands)
    return new.reshape(CH, LEV, ROWS), imported


def solution(mesh):
    in_specs = (
        P(None, None, ("comp", "dom")),
        P(None, ("comp", "dom")),
        P(None, ("comp", "dom")),
        P(("comp", "dom")),
        P(None, ("comp", "dom")),
        P(("comp", "dom")),
        P(("comp", "dom"), None),
        P(("comp", "dom")),
        P(("comp", "dom")),
    )
    out_specs = (P(None, None, ("comp", "dom")), P(None, ("comp", "dom")))
    return jax.shard_map(shards, mesh=mesh, in_specs=in_specs, out_specs=out_specs, check_vma=False)
```

```python
import math

import jax
import jax.numpy as jnp
import numpy as np
from jax import lax
from jax.experimental import pallas as pl
from jax.experimental.pallas import tpu as pltpu
from jax.sharding import PartitionSpec as P

CH = 4
LEV = 64
ROWS = 1024
HW = 512
BLK = 256
NB = ROWS // BLK
SPAN = BLK + 2 * HW
OWNERS = 64
PLANE = 16
ENT = 8192
SLAB = 1024
TAIL = 16
MESH = pl.DeviceIdType.MESH
BF = jnp.bfloat16
F32 = jnp.float32


def derivative():
    nodes = np.array([-1.0, -1.0 / math.sqrt(5.0), 1.0 / math.sqrt(5.0), 1.0])
    weights = np.ones(4)
    for column in range(4):
        for middle in range(4):
            if middle != column:
                weights[column] = weights[column] / (nodes[column] - nodes[middle])
    table = np.zeros((4, 4))
    for target in range(4):
        for column in range(4):
            if column != target:
                table[target, column] = weights[column] / weights[target] / (nodes[target] - nodes[column])
        table[target, target] = -np.sum(table[target])
    return table


def element_table():
    d = derivative()
    along_x = np.kron(np.eye(4), d)
    along_y = np.kron(d, np.eye(4))
    return jnp.asarray(-0.04 * np.concatenate([np.tile(along_x.T, (1, 16)), np.tile(along_y.T, (1, 16))]), F32)


def index(shape, dim):
    return lax.broadcasted_iota(jnp.int32, shape, dim)


def ones_where(mask):
    return jnp.where(mask, 1.0, 0.0)


def vertical(rows):
    r, c = index((rows, rows), 0), index((rows, rows), 1)
    level = r & (LEV - 1)
    up = ones_where((c == r + 1) & (level < LEV - 1))
    down = ones_where((c == r - 1) & (level > 0))
    here = ones_where(c == r) * (ones_where(level < LEV - 1) + ones_where(level > 0))
    return (up + down - here).astype(BF)


def dot(a, b):
    return lax.dot_general(a, b, (((1,), (0,)), ((), ())), preferred_element_type=F32)


def dot_t(a, b):
    return lax.dot_general(a, b, (((1,), (1,)), ((), ())), preferred_element_type=F32)


def body(
    state_in, links_in, lw_in, mass_in, flow_in, src_in, owner_in, row_in, w_in, kxy_in,
    out_ref, imp_ref,
    links_ref, lw_ref, mass_ref, flow_ref, src_ref, owner_ref, row_ref, w_ref, kxy_ref,
    load_sem, vert_ref, meta, wind, ext1, ext2, mixm, badv, ab,
    table, keys, values_ref, send, recv, row_send, row_recv, before, after, sums, imps, relay,
    halo_send, halo_recv, deep_send, deep_recv, relay_recv, forward_send, plane_send, plane_recv, line_send, line_recv, end_send, end_recv,
):
    comp = lax.axis_index("comp")
    me = lax.axis_index("dom")
    other = 1 - comp
    mz, my, mx = me // 16, lax.rem(me // 4, 4), lax.rem(me, 4)
    row = me - mx
    right = lax.rem(me + 1, OWNERS)
    left = lax.rem(me + OWNERS - 1, OWNERS)
    next_row = lax.rem(row + 4, OWNERS)
    previous_row = lax.rem(row + OWNERS - 4, OWNERS)

    def plane(q, sign):
        dz, dy = q // 4, lax.rem(q, 4)
        return lax.rem(mz + sign * dz + 4, 4) * 16 + lax.rem(my + sign * dy + 4, 4) * 4 + mx

    mid = slice(ROWS, 2 * ROWS)

    pairs = (
        (state_in, ext1.at[:, mid]), (src_in, src_ref), (row_in, row_ref), (owner_in, owner_ref), (w_in, w_ref),
        (flow_in, flow_ref), (mass_in, mass_ref), (lw_in, lw_ref), (links_in, links_ref), (kxy_in, kxy_ref),
    )
    loads = [pltpu.make_async_copy(a, b, load_sem.at[i]) for i, (a, b) in enumerate(pairs)]
    for copy in loads:
        copy.start()
    barrier = pltpu.get_barrier_semaphore()

    def greet(q, carry):
        pl.semaphore_signal(barrier, inc=1, device_id=(other, plane(q, -1)), device_id_type=MESH)
        return carry

    for side in (left, right):
        pl.semaphore_signal(barrier, inc=1, device_id=(comp, side), device_id_type=MESH)
    for k in range(1, 4):
        pl.semaphore_signal(barrier, inc=1, device_id=(comp, row + lax.rem(mx + k, 4)), device_id_type=MESH)

    @pl.when(mx == 0)
    def _():
        for k in range(4):
            pl.semaphore_signal(barrier, inc=1, device_id=(comp, previous_row + k), device_id_type=MESH)
        pl.semaphore_signal(barrier, inc=1, device_id=(comp, next_row), device_id_type=MESH)

    @pl.when(mx == 3)
    def _():
        for k in range(4):
            pl.semaphore_signal(barrier, inc=1, device_id=(comp, next_row + k), device_id_type=MESH)
        pl.semaphore_signal(barrier, inc=1, device_id=(comp, previous_row + 3), device_id_type=MESH)

    lax.fori_loop(0, PLANE, greet, 0)

    def halo(ext, width, number):
        own = ext.shape[1] - 2 * width
        copies = []
        for side, src, dst, k in (
            (right, slice(own, own + width), slice(0, width), 0),
            (left, slice(width, 2 * width), slice(own + width, own + 2 * width), 1),
        ):
            copies.append(
                pltpu.make_async_remote_copy(
                    src_ref=ext.at[:, src],
                    dst_ref=ext.at[:, dst],
                    send_sem=halo_send.at[number, k],
                    recv_sem=halo_recv.at[number, k],
                    device_id=(comp, side),
                    device_id_type=MESH,
                )
            )
        return copies

    for copy in loads:
        copy.wait()

    meta[0:8, HW : HW + ROWS] = links_ref[...].astype(F32)
    meta[8:16, HW : HW + ROWS] = lw_ref[...]
    wind[:, mid] = jnp.concatenate([flow_ref[...], jnp.zeros((6, ROWS), F32)], axis=0)
    meta[16:24, HW : HW + ROWS] = jnp.concatenate(
        [mass_ref[...], flow_ref[...], jnp.zeros((5, ROWS), F32)], axis=0
    )
    element = index((16, BLK), 1) >> 4

    def factors(blocks):
        for b in blocks:
            cols = slice(b * BLK, (b + 1) * BLK)
            total = jnp.sum(meta[8:16, cols], axis=0, keepdims=True)
            mass = meta[16:17, cols]

            @pl.when(comp == 0)
            def _():
                inv = 1.0 / (mass + total)
                ab[0:1, cols] = mass * inv
                ab[1:2, cols] = inv

            @pl.when(comp == 1)
            def _():
                half = 0.5 / mass
                ab[0:1, cols] = 1.0 - half * total
                ab[1:2, cols] = half
                ab[2:3, cols] = 0.25 * meta[17:18, cols] * meta[17:18, cols]

    def slopes(blocks):
        for g in blocks:
            cols = slice(g * BLK, (g + 1) * BLK)
            slope = kxy_ref[0:16, :] * wind[0:1, cols] + kxy_ref[16:32, :] * wind[1:2, cols]
            for p in range(BLK // 16):
                badv[g, p * 16 : p * 16 + 16, :] = jnp.where(element == p, slope, 0.0).astype(BF)

    def combine(blocks):
        for b in blocks:
            cols = slice(b * BLK, (b + 1) * BLK)
            for k in range(SPAN // BLK):
                rows = slice(k * BLK, (k + 1) * BLK)
                part = mixm[b, rows, :]
                value = part.astype(F32) + dot(badv[b + k], part)
                if k == 2:
                    value = value + ab[0:1, cols] * badv[b + 2].astype(F32)
                mixm[b, rows, :] = value.astype(BF)

    own_blocks = range(2, 2 + NB)

    at_start, at_end = mx == 0, mx == 3
    pl.semaphore_wait(barrier, jnp.where(at_start | at_end, PLANE + 8, PLANE + 7))
    small_halo = halo(meta, HW, 0) + halo(wind, ROWS, 1)
    half_rows = CH * LEV // 2
    sides = ((right, slice(0, ROWS)), (left, slice(2 * ROWS, 3 * ROWS)))

    def deep(half, k):
        rows = slice(half * half_rows, (half + 1) * half_rows)
        side, dst = sides[k]
        return pltpu.make_async_remote_copy(
            src_ref=state_in.at[rows], dst_ref=ext1.at[rows, dst],
            send_sem=deep_send.at[half, k], recv_sem=deep_recv.at[half, k],
            device_id=(comp, side), device_id_type=MESH,
        )

    def to_relay(k):
        return pltpu.make_async_remote_copy(
            src_ref=state_in.at[half_rows : 2 * half_rows], dst_ref=relay,
            send_sem=deep_send.at[1, k], recv_sem=relay_recv.at[k],
            device_id=(comp, next_row + 3 if k == 0 else previous_row), device_id_type=MESH,
        )

    def from_relay(k):
        return pltpu.make_async_remote_copy(
            src_ref=relay, dst_ref=ext1.at[half_rows : 2 * half_rows, sides[k][1]],
            send_sem=forward_send, recv_sem=deep_recv.at[1, k],
            device_id=(comp, row if k == 0 else row + 3), device_id_type=MESH,
        )

    for copy in small_halo:
        copy.start()
    for k, edge in ((0, at_end), (1, at_start)):
        pl.when(edge)(to_relay(k).start)
    for k in range(2):
        deep(0, k).start()
    for k, edge in ((0, at_end), (1, at_start)):
        pl.when(jnp.logical_not(edge))(deep(1, k).start)

    for ch in range(CH):
        line = ext1[ch * LEV : ch * LEV + 1, mid].astype(F32)
        for hi in range(8):
            table[ch * 8 + hi : ch * 8 + hi + 1, :] = line[:, hi * 128 : (hi + 1) * 128]
    source = src_ref[...]
    target = row_ref[...]
    owner = owner_ref[...]
    relative = (
        jnp.bitwise_and(lax.shift_right_logical(owner, 4) - mz + 4, 3) * 16
        + jnp.bitwise_and(lax.shift_right_logical(owner, 2) - my + 4, 3) * 4
        + jnp.bitwise_and(owner, 3)
    )
    first = relative * 8 + lax.shift_right_logical(target, 7)
    keys[0] = jnp.bitwise_and(source, 127).astype(F32)
    keys[1] = lax.shift_right_logical(source, 7).astype(F32)
    keys[2] = jnp.bitwise_and(target, 127).astype(F32)
    keys[3] = first.astype(F32)
    keys[4] = (first - 256).astype(F32)
    sub = index((8, 16, SLAB), 0) * 16 + index((8, 16, SLAB), 1)
    lanes = sub.astype(F32).astype(BF)
    upper = (sub + 128).astype(F32).astype(BF)
    high = index((8, SLAB), 0).astype(F32)
    exported = table[...].astype(BF)
    one, zero = jnp.asarray(1.0, BF), jnp.asarray(0.0, BF)
    chunks = SLAB // 128

    def row_of(which, i):
        return jnp.concatenate([keys[which, pl.ds(i * chunks + k, 1), :] for k in range(chunks)], axis=1)

    def wide(x):
        return jnp.broadcast_to(x, (16, SLAB)).astype(BF)[None]

    def spots(which, i):
        key = wide(row_of(which, i))
        return jnp.concatenate(
            [jnp.where(part == key, one, zero).reshape(128, SLAB) for part in (lanes, upper)], axis=0
        )

    def first_part(i, total):
        hot = jnp.where(lanes == wide(row_of(0, i)), one, zero).reshape(128, SLAB)
        found = dot(exported, hot)
        chosen = high == row_of(1, i)
        weight = jnp.concatenate([w_ref[pl.ds(i * chunks + k, 1), :] for k in range(chunks)], axis=1)
        low = lanes == wide(row_of(2, i))
        rows = []
        for ch in range(CH):
            value = jnp.sum(jnp.where(chosen, found[ch * 8 : ch * 8 + 8], 0.0), axis=0, keepdims=True) * weight
            rows.append(jnp.where(low, wide(value), zero).reshape(128, SLAB))
        values = jnp.concatenate(rows, axis=0)
        values_ref[i] = values
        return total + dot_t(spots(3, i), values)

    def second_part(i, total):
        return total + dot_t(spots(4, i), values_ref[i])

    half_owners = OWNERS // 2

    def pack(part, total):
        for pair in range(2):
            parts = [
                total[:, c * 128 : (c + 1) * 128].reshape(half_owners, 8, 128) for c in (2 * pair, 2 * pair + 1)
            ]
            send[part * half_owners : (part + 1) * half_owners, pair * 16 : pair * 16 + 16, :] = jnp.concatenate(
                parts, axis=1
            ).astype(BF)

    def post(part):
        def one_post(q, carry):
            pltpu.make_async_remote_copy(
                src_ref=send.at[pl.ds(q * 4, 4)],
                dst_ref=recv.at[pl.ds(q * 4, 4)],
                send_sem=plane_send.at[part],
                recv_sem=plane_recv.at[part],
                device_id=(other, plane(q, 1)),
                device_id_type=MESH,
            ).start()
            return carry

        lax.fori_loop(part * PLANE // 2, (part + 1) * PLANE // 2, one_post, 0)

    start = jnp.zeros((256, CH * 128), F32)
    pack(0, lax.fori_loop(0, ENT // SLAB, first_part, start, unroll=True))
    post(0)
    pack(1, lax.fori_loop(0, ENT // SLAB, second_part, start, unroll=True))
    post(1)

    base_iota = index((128, BLK), 0).astype(F32).astype(BF).reshape(8, 16, BLK)

    def build(slots, blocks):
        for b in blocks:
            cols = slice(b * BLK, (b + 1) * BLK)
            place = meta[0:8, cols] + (index((8, BLK), 1) + HW).astype(F32)
            weights = [
                jnp.broadcast_to(meta[8 + s : 9 + s, cols] * ab[1:2, cols], (16, BLK)).astype(BF)[None] for s in range(slots)
            ]

            def piece(k, carry):
                key = place - (k * 128).astype(F32)
                total = jnp.zeros((8, 16, BLK), BF)
                for s in range(slots):
                    spot = jnp.broadcast_to(key[s : s + 1], (16, BLK)).astype(BF)[None]
                    total = total + jnp.where(base_iota == spot, weights[s], zero)
                mixm[b, pl.ds(pl.multiple_of(k * 128, 128), 128), :] = total.reshape(128, BLK)
                return carry

            lax.fori_loop(0, SPAN // 128, piece, 0)

    vert_ref[...] = vertical(CH * LEV)
    factors(own_blocks)

    @pl.when(comp == 0)
    def _():
        slopes(range(NB, 2 * NB))
        build(3, own_blocks)

    pl.when(comp == 1)(lambda: build(7, own_blocks))
    for k, edge in ((0, at_end), (1, at_start)):

        @pl.when(edge)
        def _():
            to_relay(k).wait_recv()
            from_relay(k).start()

    for copy in small_halo:
        copy.wait()
    outer = (0, 1, 6, 7)
    factors(outer)

    @pl.when(comp == 0)
    def _():
        slopes((0, 1, 2, 3, 8, 9, 10, 11))
        build(3, outer)
        combine(range(2 * NB))

    pl.when(comp == 1)(lambda: build(7, outer))

    def settled(window, own, b, vmat):
        cols = slice(b * BLK, (b + 1) * BLK)
        value = ab[0:1, cols] * own.astype(F32) + dot(window, mixm[b])
        if vmat is not None:
            value = value + ab[2:3, cols] * dot(vmat, own)
        return value

    def first_step(ext, b, vmat):
        own = ext[:, HW + b * BLK : HW + (b + 1) * BLK]
        return settled(ext[:, b * BLK : b * BLK + SPAN], own, b, vmat)

    def second_step(ext, j, vmat):
        own = ext[:, HW + j * BLK : HW + (j + 1) * BLK]
        return settled(ext[:, j * BLK : j * BLK + SPAN], own, j + 2, vmat)

    def arrived(part):
        rows = slice(part * half_owners, (part + 1) * half_owners)
        return pltpu.make_async_remote_copy(
            src_ref=send.at[rows], dst_ref=recv.at[rows], send_sem=plane_send.at[part], recv_sem=plane_recv.at[part],
            device_id=(other, me), device_id_type=MESH,
        )

    total = jnp.zeros((4, CH * 8, 128), F32)
    for part in range(2):
        arrived(part).wait_recv()
        rows = slice(part * half_owners, (part + 1) * half_owners)
        total = total + jnp.sum(recv[rows].astype(F32).reshape(PLANE // 2, 4, CH * 8, 128), axis=0)
    row_send[...] = total.astype(BF)
    line = []
    for k in range(1, 4):
        line.append(
            pltpu.make_async_remote_copy(
                src_ref=row_send, dst_ref=row_recv.at[k - 1], send_sem=line_send.at[k - 1], recv_sem=line_recv.at[k - 1],
                device_id=(comp, row + lax.rem(mx + k, 4)), device_id_type=MESH,
            )
        )

    def end(which, slot, target, source, k):
        return pltpu.make_async_remote_copy(
            src_ref=row_send.at[source], dst_ref=which.at[slot], send_sem=end_send.at[k], recv_sem=end_recv.at[k, slot],
            device_id=(comp, target), device_id_type=MESH,
        )

    ends = [end(before, mx, next_row, 3, 0), end(after, mx, previous_row + 3, 0, 1)]
    for copy in ends + line:
        copy.start()

    for half in range(2):
        for k in range(2):
            deep(half, k).wait()
    for copy in line:
        copy.wait()
    total = row_send[...].astype(F32)
    for k in range(3):
        total = total + row_recv[k].astype(F32)
    sums[1:5] = total

    @pl.when(mx == 0)
    def _():
        for k in range(4):
            end(before, k, next_row, 3, 0).wait_recv()
        sums[0] = jnp.sum(before[...].astype(F32), axis=0)

    @pl.when(mx == 3)
    def _():
        for k in range(4):
            end(after, k, previous_row + 3, 0, 1).wait_recv()
        sums[5] = jnp.sum(after[...].astype(F32), axis=0)

    for side in range(3):
        block = sums[mx + side]
        for ch in range(CH):
            for hi in range(8):
                cols = slice(side * ROWS + hi * 128, side * ROWS + (hi + 1) * 128)
                imps[ch : ch + 1, cols] = block[ch * 8 + hi : ch * 8 + hi + 1, :]
    imp_ref[...] = imps[0:CH, mid]
    top = index((TAIL, BLK), 0)

    for g in range(3 * NB):
        cols = slice(g * BLK, (g + 1) * BLK)
        for ch in range(CH):
            rows = slice(ch * LEV, ch * LEV + TAIL)
            old = ext1[rows, cols].astype(F32)
            new = old + 0.5 * (imps[ch : ch + 1, cols] - old)
            ext1[rows, cols] = jnp.where(top == 0, new, old).astype(BF)

    def steps(vmat):
        for b in range(2 * NB):
            ext2[:, b * BLK : (b + 1) * BLK] = first_step(ext1, b, vmat).astype(BF)
        for j in range(NB):
            out_ref[:, j * BLK : (j + 1) * BLK] = second_step(ext2, j, vmat).astype(BF)

    pl.when(comp == 0)(lambda: steps(None))
    pl.when(comp == 1)(lambda: steps(vert_ref[...]))
    pl.when(at_end)(from_relay(0).wait_send)
    pl.when(at_start)(from_relay(1).wait_send)
    for copy in ends:
        copy.wait_send()
    arrived(0).wait_send()
    arrived(1).wait_send()


def publish(new_in, imp_in, new_out, imp_out):
    new_out[...] = new_in[...]
    imp_out[...] = imp_in[...]


def shards(state, links, link_weight, point_mass, flow, ov_src, ov_owner, ov_row, ov_weight):
    hbm = pl.BlockSpec(memory_space=pl.ANY)
    vm = pl.BlockSpec(memory_space=pltpu.VMEM)
    operands = (
        state.reshape(CH * LEV, ROWS),
        links,
        link_weight,
        point_mass.reshape(1, ROWS),
        flow,
        ov_src.reshape(ENT // 128, 128),
        ov_owner.reshape(ENT // 128, 128),
        ov_row.reshape(ENT // 128, 128),
        ov_weight.reshape(ENT // 128, 128),
        element_table(),
    )
    new, imported = pl.pallas_call(
        body,
        out_shape=(
            jax.ShapeDtypeStruct((CH * LEV, ROWS), BF),
            jax.ShapeDtypeStruct((CH, ROWS), F32),
        ),
        in_specs=[hbm] * 10,
        out_specs=(vm, vm),
        scratch_shapes=[pltpu.VMEM(x.shape, x.dtype) for x in operands[1:]]
        + [
            pltpu.SemaphoreType.DMA((10,)),
            pltpu.VMEM((CH * LEV, CH * LEV), BF),
            pltpu.VMEM((24, 2 * ROWS), F32),
            pltpu.VMEM((8, 3 * ROWS), F32),
            pltpu.VMEM((CH * LEV, 3 * ROWS), BF),
            pltpu.VMEM((CH * LEV, 2 * ROWS), BF),
            pltpu.VMEM((2 * NB, SPAN, BLK), BF),
            pltpu.VMEM((3 * NB, BLK, BLK), BF),
            pltpu.VMEM((8, 2 * ROWS), F32),
            pltpu.VMEM((CH * 8, 128), F32),
            pltpu.VMEM((5, ENT // 128, 128), F32),
            pltpu.VMEM((ENT // SLAB, CH * 128, SLAB), BF),
            pltpu.VMEM((OWNERS, CH * 8, 128), BF),
            pltpu.VMEM((OWNERS, CH * 8, 128), BF),
            pltpu.VMEM((4, CH * 8, 128), BF),
            pltpu.VMEM((3, 4, CH * 8, 128), BF),
            pltpu.VMEM((4, CH * 8, 128), BF),
            pltpu.VMEM((4, CH * 8, 128), BF),
            pltpu.VMEM((6, CH * 8, 128), F32),
            pltpu.VMEM((8, 3 * ROWS), F32),
            pltpu.VMEM((CH * LEV // 2, ROWS), BF),
            pltpu.SemaphoreType.DMA((2, 2)),
            pltpu.SemaphoreType.DMA((2, 2)),
            pltpu.SemaphoreType.DMA((2, 2)),
            pltpu.SemaphoreType.DMA((2, 2)),
            pltpu.SemaphoreType.DMA((2,)),
            pltpu.SemaphoreType.DMA,
            pltpu.SemaphoreType.DMA((2,)),
            pltpu.SemaphoreType.DMA((2,)),
            pltpu.SemaphoreType.DMA((3,)),
            pltpu.SemaphoreType.DMA((3,)),
            pltpu.SemaphoreType.DMA((2,)),
            pltpu.SemaphoreType.DMA((2, 4)),
        ],
        compiler_params=pltpu.CompilerParams(
            collective_id=0, has_side_effects=True, vmem_limit_bytes=56 * 1024 * 1024
        ),
        name="coupled",
    )(*operands)
    cut = 1
    parts = [pl.BlockSpec((CH * LEV // cut, ROWS), lambda i: (i, 0)), pl.BlockSpec((CH, ROWS), lambda i: (0, 0))]
    new, imported = pl.pallas_call(
        publish,
        out_shape=(
            jax.ShapeDtypeStruct((CH * LEV, ROWS), BF),
            jax.ShapeDtypeStruct((CH, ROWS), F32),
        ),
        grid=(cut,),
        in_specs=parts,
        out_specs=parts,
        compiler_params=pltpu.CompilerParams(vmem_limit_bytes=56 * 1024 * 1024),
        name="publish",
    )(new, imported)
    return new.reshape(CH, LEV, ROWS), imported


def solution(mesh):
    in_specs = (
        P(None, None, ("comp", "dom")),
        P(None, ("comp", "dom")),
        P(None, ("comp", "dom")),
        P(("comp", "dom")),
        P(None, ("comp", "dom")),
        P(("comp", "dom")),
        P(("comp", "dom"), None),
        P(("comp", "dom")),
        P(("comp", "dom")),
    )
    out_specs = (P(None, None, ("comp", "dom")), P(None, ("comp", "dom")))
    return jax.shard_map(shards, mesh=mesh, in_specs=in_specs, out_specs=out_specs, check_vma=False)
```
